32 devices in a mesh: grp: 4 (over z), wide: 4 (over x, core), blk: 2 (over y).
Axes of the slice: x: 2, y: 2, z: 4, core: 2. Of those that a mesh axis runs over, the one named last changes fastest.
Arguments:
- activations: bfloat16 [2048, 8192], P('blk', ('grp', 'wide')), may hold values from -6 to 6
- out_grads: bfloat16 [2048, 8192], P('blk', ('grp', 'wide')), may hold values from -6 to 6
- in_projection: bfloat16 [8192, 32], P(('grp', 'wide')), may hold values from -0.0625 to 0.0625
- out_projection: bfloat16 [8192, 64], P(('grp', 'wide')), may hold values from -0.0625 to 0.0625
- in_inverse: float32 [32, 32], replicated, may hold values from -1 to 1
- out_inverse: float32 [64, 64], replicated, may hold values from -0.75 to 0.75
- grad_store: bfloat16 [49152, 2048], P(('grp', 'wide', 'blk')), may hold values from -0.0234375 to 0.0234375
Outputs:
- influence: float32 [64, 49152], P(None, ('grp', 'wide', 'blk'))
The draws below stay inside these ranges and needn't reach their ends.
All inputs are finite; a program needn't handle non-finite values.
Results may differ from the reference program's by a relative error of at most 0.0029.
Values may be sent and summed in bfloat16 or wider, within the bound.
No kernel may reach another device: no remote copies, remote signals or barrier semaphores. Data moves between devices by JAX's collectives and lax.ppermute only.
A program may use at most 64 MiB of HBM per device.

```python
import jax
import jax.numpy as jnp
from jax import lax

D = 8192
SEQ = 32
K_IN = 32
K_OUT = 64
QUERIES = 64
TOKENS = 2048
KDIM = 2048
ROWS = 49152


def block_levels(stream_key, shape, split, low, top_value):
    level = 1.0
    for position, parts in split:
        draws = jax.random.uniform(jax.random.fold_in(jax.random.fold_in(stream_key, 6), position), (parts,), jnp.float32, low / len(split), top_value / len(split))
        level = level * jnp.repeat(jnp.exp(draws), shape[position] // parts).reshape((-1,) + (1,) * (len(shape) - 1 - position))
    return level


def normal_values(own_key, extent, width, most, shards=(), kind=jnp.bfloat16):
    loudness = block_levels(own_key, extent, shards, -0.22, 0.18) if shards else 1.0
    entries = jax.random.normal(own_key, extent, jnp.float32) * width * loudness
    return jnp.minimum(jnp.maximum(entries, -most), most).astype(kind)


def setup_inputs(seed: int = 0) -> dict:
    seeds = jax.random.split(jax.random.key(seed), 8)
    activations = normal_values(seeds[0], (TOKENS, D), 1.0, 6.0, ((0, 2), (1, 16)))
    out_grads = normal_values(seeds[1], (TOKENS, D), 1.0, 6.0, ((0, 2), (1, 16)))
    in_projection = normal_values(seeds[2], (D, K_IN), D ** -0.5, 0.0625, ((0, 16),))
    out_projection = normal_values(seeds[3], (D, K_OUT), D ** -0.5, 0.0625, ((0, 16),))
    in_inverse = normal_values(seeds[4], (K_IN, K_IN), K_IN ** -0.5, 1.0, (), jnp.float32)
    out_inverse = normal_values(seeds[5], (K_OUT, K_OUT), K_OUT ** -0.5, 0.75, (), jnp.float32)
    grad_store = normal_values(seeds[6], (ROWS, KDIM), (SEQ * KDIM) ** -0.5, 0.0234375, ((0, 32),))
    return {"activations": activations, "out_grads": out_grads, "in_projection": in_projection, "out_projection": out_projection, "in_inverse": in_inverse, "out_inverse": out_inverse, "grad_store": grad_store}


highest = lax.Precision.HIGHEST


def reference(activations, out_grads, in_projection, out_projection, in_inverse, out_inverse, grad_store):
    low_input = jnp.dot(activations, in_projection, preferred_element_type=jnp.float32)
    low_output = jnp.dot(out_grads, out_projection, preferred_element_type=jnp.float32)
    low_input = low_input.reshape(QUERIES, SEQ, K_IN)
    low_output = low_output.reshape(QUERIES, SEQ, K_OUT)
    gradient = jnp.einsum("qso,qsi->qoi", low_output, low_input, precision=highest)
    shaped = jnp.einsum("ao,qoi->qai", out_inverse, gradient, precision=highest)
    shaped = jnp.einsum("qai,ib->qab", shaped, in_inverse, precision=highest)
    queries = shaped.reshape(QUERIES, KDIM).astype(jnp.bfloat16)
    return lax.dot_general(queries, grad_store, (((1,), (1,)), ((), ())), preferred_element_type=jnp.float32)
```

```python
import functools

import jax
import jax.numpy as jnp
from jax import lax
from jax.experimental import pallas as pl
from jax.experimental.pallas import tpu as pltpu
from jax.sharding import PartitionSpec as P

SEQ = 32
VMEM = pl.BlockSpec(memory_space=pltpu.VMEM)
HBM = pl.BlockSpec(memory_space=pl.ANY)
MIB = 1 << 20


def contract(lhs, rhs, left, right):
    return lax.dot_general(
        lhs, rhs, (((left,), (right,)), ((), ())), preferred_element_type=jnp.float32
    )


def two_parts(value):
    high = value.astype(jnp.bfloat16)
    return high, (value - high.astype(jnp.float32)).astype(jnp.bfloat16)


def project_kernel(flip, acts, grads, in_proj, out_proj, out, act_buf, grad_buf, sems):
    slices, tokens = act_buf.shape[0], act_buf.shape[1]
    width_in = in_proj.shape[0]
    mine = lax.axis_index("wide")
    copies = []
    for k in range(slices):
        rows = pl.ds(pl.multiple_of((mine ^ (flip + 2 * k)) * tokens, tokens), tokens)
        for source, target, part in ((acts, act_buf, 0), (grads, grad_buf, 1)):
            copy = pltpu.make_async_copy(source.at[rows], target.at[k], sems.at[k, part])
            copy.start()
            copies.append(copy)
    for k in range(slices):
        copies[2 * k].wait()
        out[k, :width_in] = contract(in_proj[...], act_buf[k], 1, 1)
        copies[2 * k + 1].wait()
        out[k, width_in:] = contract(out_proj[...], grad_buf[k], 1, 1)


def project(flip, shards, acts, grads, in_proj, out_proj):
    tokens, features = acts.shape[0] // shards, acts.shape[1]
    slices = shards // 2
    width = in_proj.shape[0] + out_proj.shape[0]
    return pl.pallas_call(
        functools.partial(project_kernel, flip),
        out_shape=jax.ShapeDtypeStruct((slices, width, tokens), jnp.float32),
        in_specs=[HBM, HBM, VMEM, VMEM],
        out_specs=VMEM,
        scratch_shapes=[
            pltpu.VMEM((slices, tokens, features), jnp.bfloat16),
            pltpu.VMEM((slices, tokens, features), jnp.bfloat16),
            pltpu.SemaphoreType.DMA((slices, 2)),
        ],
        compiler_params=pltpu.CompilerParams(vmem_limit_bytes=8 * MIB),
        cost_estimate=pl.CostEstimate(
            flops=2 * slices * tokens * features * width,
            bytes_accessed=4 * slices * tokens * features,
            transcendentals=0,
        ),
    )(acts, grads, in_proj, out_proj)


def spread_kernel(in_inverse, out_inverse, spread_out, spread_in):
    width_out, width_in = out_inverse.shape[0], in_inverse.shape[0]
    columns, lanes = spread_out.shape[1], spread_in.shape[1]
    row = lax.broadcasted_iota(jnp.int32, (width_out, columns), 0)
    column = lax.broadcasted_iota(jnp.int32, (width_out, columns), 1)
    start = row * width_in
    repeat = ((column >= start) & (column < start + width_in)).astype(jnp.bfloat16)
    high, low = two_parts(out_inverse[...])
    high = contract(high, repeat, 0, 0).astype(jnp.bfloat16)
    low = contract(low, repeat, 0, 0).astype(jnp.bfloat16)
    spread_out[...] = jnp.concatenate([high, low, high, low], axis=0)
    row = lax.broadcasted_iota(jnp.int32, (width_in, lanes), 0)
    column = lax.broadcasted_iota(jnp.int32, (width_in, lanes), 1)
    tile = (lax.rem(column, width_in) == row).astype(jnp.bfloat16)
    high, low = two_parts(in_inverse[...])
    high = contract(high, tile, 1, 0).astype(jnp.bfloat16)
    low = contract(low, tile, 1, 0).astype(jnp.bfloat16)
    spread_in[...] = jnp.concatenate([high, low, high, low], axis=0)


def spread_inverses(in_inverse, out_inverse):
    width_in, width_out = in_inverse.shape[0], out_inverse.shape[0]
    return pl.pallas_call(
        spread_kernel,
        out_shape=(
            jax.ShapeDtypeStruct((4 * width_out, width_out * width_in), jnp.bfloat16),
            jax.ShapeDtypeStruct((4 * width_in, 128), jnp.bfloat16),
        ),
        in_specs=[VMEM, VMEM],
        out_specs=(VMEM, VMEM),
        compiler_params=pltpu.CompilerParams(vmem_limit_bytes=8 * MIB),
    )(in_inverse, out_inverse)


def query_kernel(held, got, spread_out, spread_in, out):
    width_in = spread_in.shape[0] // 4
    tokens = held.shape[1]
    queries, columns = out.shape
    lanes = spread_in.shape[1]
    low = (held[...] + got[...]).T
    in_high, in_low = two_parts(low[:, :width_in])
    out_high, out_low = two_parts(low[:, width_in:])
    side_in = jnp.concatenate([in_high, in_high, in_low, in_low], axis=1)
    side_out = jnp.concatenate([out_high, out_high, out_low, out_low], axis=1)
    spread_in_low = contract(side_in, spread_in[...], 1, 0)
    step = 256
    wide = jnp.concatenate([spread_in_low] * (step // lanes), axis=1)
    for start in range(0, columns, step):
        part = contract(side_out, spread_out[:, start : start + step], 1, 0) * wide
        part = jnp.sum(part.reshape(queries, tokens // queries, step), axis=1)
        out[:, start : start + step] = part.astype(out.dtype)


def build_queries(held, got, spread_out, spread_in):
    tokens = held.shape[1]
    return pl.pallas_call(
        query_kernel,
        out_shape=jax.ShapeDtypeStruct((tokens // SEQ, spread_out.shape[1]), jnp.bfloat16),
        in_specs=[VMEM] * 4,
        out_specs=VMEM,
        compiler_params=pltpu.CompilerParams(vmem_limit_bytes=12 * MIB),
    )(held, got, spread_out, spread_in)


def score_kernel(wide, blocks, queries, store, out):
    mine = lax.axis_index("blk")
    group = out.shape[0] // (blocks * wide)
    step = 256
    for start in range(0, out.shape[1], step):
        part = contract(queries[...], store[start : start + step], 1, 1)
        for w in range(wide):
            for s in range(blocks):
                source = (w * blocks + s) * group
                target = pl.multiple_of(((mine ^ s) * wide + w) * group, group)
                out[pl.ds(target, group), start : start + step] = part[source : source + group]


def scores(wide, blocks, queries, store):
    return pl.pallas_call(
        functools.partial(score_kernel, wide, blocks),
        out_shape=jax.ShapeDtypeStruct((queries.shape[0], store.shape[0]), jnp.float32),
        in_specs=[VMEM, VMEM],
        out_specs=VMEM,
        compiler_params=pltpu.CompilerParams(vmem_limit_bytes=20 * MIB),
    )(queries, store)


def exchange(value, axis, bit, size):
    return lax.ppermute(value, axis, [(i, i ^ bit) for i in range(size)])


def on_device(
    sizes, activations, out_grads, in_projection, out_projection, in_inverse, out_inverse, grad_store
):
    wide, groups, blocks = sizes["wide"], sizes["grp"], sizes["blk"]
    in_proj, out_proj = in_projection.T, out_projection.T
    given = project(1, wide, activations, out_grads, in_proj, out_proj)
    got = exchange(given, "wide", 1, wide)
    held = project(0, wide, activations, out_grads, in_proj, out_proj)
    held = held + got
    bit = 2
    while bit < wide:
        half = held.shape[0] // 2
        held = held[:half] + exchange(held[half:], "wide", bit, wide)
        bit *= 2
    held = held[0]
    bit = 1
    got = jnp.zeros_like(held)
    while bit < groups:
        if bit > 1:
            held = held + got
        got = exchange(held, "grp", bit, groups)
        bit *= 2
    spread_out, spread_in = spread_inverses(in_inverse, out_inverse)
    queries = build_queries(held, got, spread_out, spread_in)
    bit = 1
    while bit < blocks:
        queries = jnp.concatenate([queries, exchange(queries, "blk", bit, blocks)], axis=0)
        bit *= 2
    queries = lax.all_gather(queries, "wide", axis=0, tiled=True)
    return scores(wide, blocks, queries, grad_store)


def solution(mesh):
    return jax.shard_map(
        functools.partial(on_device, dict(mesh.shape)),
        mesh=mesh,
        in_specs=(
            P("blk", ("grp", "wide")),
            P("blk", ("grp", "wide")),
            P(("grp", "wide"), None),
            P(("grp", "wide"), None),
            P(),
            P(),
            P(("grp", "wide", "blk"), None),
        ),
        out_specs=P(None, ("grp", "wide", "blk")),
        check_vma=False,
    )
```

```python
import functools
import itertools

import jax
import jax.numpy as jnp
from jax import lax
from jax.experimental import pallas as pl
from jax.experimental.pallas import tpu as pltpu
from jax.sharding import PartitionSpec as P

SEQ = 32
VMEM = pl.BlockSpec(memory_space=pltpu.VMEM)
HBM = pl.BlockSpec(memory_space=pltpu.HBM)
MIB = 1 << 20


def contract(lhs, rhs, left, right):
    return lax.dot_general(
        lhs, rhs, (((left,), (right,)), ((), ())), preferred_element_type=jnp.float32
    )


def two_parts(value):
    high = value.astype(jnp.bfloat16)
    return high, (value - high.astype(jnp.float32)).astype(jnp.bfloat16)


def odd_bits(value):
    for shift in (16, 8, 4, 2, 1):
        value = value ^ (value >> shift)
    return value & 1


def exchange(value, sizes, wide=0, grp=0, blk=0):
    flip = odd_bits(wide) ^ odd_bits(grp >> 1)
    return swap(value, sizes, {"wide": 2 * wide + flip, "grp": grp, "blk": blk})


def swap(value, sizes, far):
    axes = tuple(sizes)
    coordinates = list(itertools.product(*(range(sizes[a]) for a in axes)))
    index = {c: i for i, c in enumerate(coordinates)}
    pairs = [
        (i, index[tuple(p ^ far.get(a, 0) for p, a in zip(c, axes))])
        for c, i in index.items()
    ]
    return lax.ppermute(value, axes, pairs)


def own_half():
    slot, group = lax.axis_index("wide"), lax.axis_index("grp")
    return lax.rem(slot, 2) ^ odd_bits(slot // 2) ^ odd_bits(group // 2)


def project_kernel(
    lows, width_in, acts, grads, proj, given, kept, act_buf, grad_buf, sems
):
    slices, spans = given.shape[0], given.shape[0] // lows
    tokens = given.shape[2]
    half = own_half()
    x, low = lax.axis_index("wide") // 2, lax.rem(lax.axis_index("grp"), lows)
    copies = []
    for k in range(2 * spans):
        first = ((x ^ (k % spans)) * 2 + (half ^ (k < spans))) * lows * tokens
        rows = pl.ds(pl.multiple_of(first, lows * tokens), lows * tokens)
        for source, target, part in ((acts, act_buf, 0), (grads, grad_buf, 1)):
            copy = pltpu.make_async_copy(source.at[rows], target.at[k], sems.at[k, part])
            copy.start()
            copies.append(copy)
    for k in range(2 * spans):
        copies[2 * k].wait()
        copies[2 * k + 1].wait()
        low_in = contract(proj[:width_in], act_buf[k], 1, 1)
        low_out = contract(proj[width_in:], grad_buf[k], 1, 1)
        out = given if k < spans else kept
        for place in range(lows):
            slot = (k % spans) * lows + (low ^ place)
            lanes = slice(place * tokens, (place + 1) * tokens)
            out[slot, :width_in] = low_in[:, lanes]
            out[slot, width_in:] = low_out[:, lanes]


def project(slices, lows, acts, grads, proj, width_in):
    tokens, features = acts.shape[0] // (2 * slices), acts.shape[1]
    width = proj.shape[0]
    spans = slices // lows
    out = jax.ShapeDtypeStruct((slices, width, tokens), jnp.float32)
    return pl.pallas_call(
        functools.partial(project_kernel, lows, width_in),
        out_shape=(out, out),
        in_specs=[HBM] * 2 + [VMEM],
        out_specs=(VMEM, VMEM),
        scratch_shapes=[
            pltpu.VMEM((2 * spans, tokens * lows, features), jnp.bfloat16),
            pltpu.VMEM((2 * spans, tokens * lows, features), jnp.bfloat16),
            pltpu.SemaphoreType.DMA((2 * spans + 1, 2)),
        ],
        compiler_params=pltpu.CompilerParams(vmem_limit_bytes=55885824),
        cost_estimate=pl.CostEstimate(
            flops=4 * slices * tokens * features * width,
            bytes_accessed=8 * slices * tokens * features,
            transcendentals=0,
        ),
    )(acts, grads, proj)


def spread_kernel(in_inverse, out_inverse, spread_out, spread_in):
    width_out, width_in = out_inverse.shape[0], in_inverse.shape[0]
    columns, lanes = spread_out.shape[1], spread_in.shape[1]
    row = lax.broadcasted_iota(jnp.int32, (width_out, columns), 0)
    column = lax.broadcasted_iota(jnp.int32, (width_out, columns), 1)
    start = row * width_in
    repeat = ((column >= start) & (column < start + width_in)).astype(jnp.bfloat16)
    high, low = two_parts(out_inverse[...])
    high = contract(high, repeat, 0, 0).astype(jnp.bfloat16)
    low = contract(low, repeat, 0, 0).astype(jnp.bfloat16)
    spread_out[...] = jnp.concatenate([high, low, high, low], axis=0)
    row = lax.broadcasted_iota(jnp.int32, (width_in, lanes), 0)
    column = lax.broadcasted_iota(jnp.int32, (width_in, lanes), 1)
    tile = (lax.rem(column, width_in) == row).astype(jnp.bfloat16)
    high, low = two_parts(in_inverse[...])
    high = contract(high, tile, 1, 0).astype(jnp.bfloat16)
    low = contract(low, tile, 1, 0).astype(jnp.bfloat16)
    spread_in[...] = jnp.concatenate([high, low, high, low], axis=0)


def spread_inverses(in_inverse, out_inverse):
    width_in, width_out = in_inverse.shape[0], out_inverse.shape[0]
    return pl.pallas_call(
        spread_kernel,
        out_shape=(
            jax.ShapeDtypeStruct((4 * width_out, width_out * width_in), jnp.bfloat16),
            jax.ShapeDtypeStruct((4 * width_in, 128), jnp.bfloat16),
        ),
        in_specs=[VMEM, VMEM],
        out_specs=(VMEM, VMEM),
        compiler_params=pltpu.CompilerParams(vmem_limit_bytes=8 * MIB),
        cost_estimate=pl.CostEstimate(flops=1 << 33, bytes_accessed=16 * MIB, transcendentals=0),
    )(in_inverse, out_inverse)


def query_kernel(held, got, spread_out, spread_in, out):
    width_in = spread_in.shape[0] // 4
    tokens = held.shape[1]
    queries, columns = out.shape
    lanes = spread_in.shape[1]
    low = (held[...] + got[...]).T
    in_high, in_low = two_parts(low[:, :width_in])
    out_high, out_low = two_parts(low[:, width_in:])
    side_in = jnp.concatenate([in_high, in_high, in_low, in_low], axis=1)
    side_out = jnp.concatenate([out_high, out_high, out_low, out_low], axis=1)
    spread_in_low = contract(side_in, spread_in[...], 1, 0)
    step = 256
    wide = jnp.concatenate([spread_in_low] * (step // lanes), axis=1)
    for start in range(0, columns, step):
        part = contract(side_out, spread_out[:, start : start + step], 1, 0) * wide
        part = jnp.sum(part.reshape(queries, tokens // queries, step), axis=1)
        out[:, start : start + step] = part.astype(out.dtype)


def build_queries(held, got, spread_out, spread_in):
    tokens = held.shape[1]
    return pl.pallas_call(
        query_kernel,
        out_shape=jax.ShapeDtypeStruct((tokens // SEQ, spread_out.shape[1]), jnp.bfloat16),
        in_specs=[VMEM] * 4,
        out_specs=VMEM,
        compiler_params=pltpu.CompilerParams(vmem_limit_bytes=12 * MIB),
        cost_estimate=pl.CostEstimate(flops=1 << 33, bytes_accessed=16 * MIB, transcendentals=0),
    )(held, got, spread_out, spread_in)


def score_kernel(order, wide, lows, held, got, store, out):
    blk, x, half = lax.axis_index("blk"), lax.axis_index("wide") // 2, own_half()
    queries = jnp.concatenate([held[...], got[...]], axis=0)
    rows = out.shape[0] // len(order)
    targets = [
        pl.multiple_of((((blk ^ far_blk) * (wide // 2) + (x ^ far_x)) * 2 + (half ^ flip)) * rows, rows)
        for far_blk, far_x, flip in order
    ]
    step = 512
    swapped = lax.rem(lax.axis_index("grp"), lows) == 1
    for start in range(0, out.shape[1], step):
        part = contract(queries, store[start : start + step], 1, 1)
        part = part.reshape(len(order), rows, step)
        if lows > 1:
            part = jnp.where(swapped, jnp.roll(part, rows // 2, axis=1), part)
        for r, row in enumerate(targets):
            out[pl.ds(row, rows), start : start + step] = part[r]


def scores(order, wide, lows, held, got, store):
    return pl.pallas_call(
        functools.partial(score_kernel, order, wide, lows),
        out_shape=jax.ShapeDtypeStruct((2 * held.shape[0], store.shape[0]), jnp.float32),
        in_specs=[VMEM] * 3,
        out_specs=VMEM,
        compiler_params=pltpu.CompilerParams(vmem_limit_bytes=20 * MIB),
    )(held, got, store)


def stack(pieces):
    rows = pieces[0].shape[0]
    zero = jnp.zeros((), pieces[0].dtype)
    return sum(
        lax.pad(piece, zero, ((n * rows, (len(pieces) - 1 - n) * rows, 0), (0, 0, 0)))
        for n, piece in enumerate(pieces)
    )


def on_device(
    sizes, activations, out_grads, in_projection, out_projection, in_inverse, out_inverse, grad_store
):
    wide, groups, blocks = sizes["wide"], sizes["grp"], sizes["blk"]
    spans, lows = wide // 2, min(groups, 2)
    slices = spans * lows
    given, kept = project(
        slices, lows, activations, out_grads, jnp.concatenate([in_projection.T, out_projection.T], axis=0), in_inverse.shape[0]
    )
    both = kept + swap(given, sizes, {"wide": 1})
    held = both[0]
    for k in range(slices - 1, 0, -1):
        held = held + exchange(both[k], sizes, wide=k // lows, grp=k % lows)
    last = jnp.zeros_like(held)
    bit = lows
    while bit < groups:
        if bit > lows:
            held = held + last
        last = exchange(held, sizes, grp=bit)
        bit *= 2
    spread_out, spread_in = spread_inverses(in_inverse, out_inverse)
    queries = build_queries(held, last, spread_out, spread_in)
    if lows > 1:
        other = exchange(queries, sizes, grp=1)
        queries = jnp.concatenate([queries, other], axis=0)
    order = [(0, 0)]
    bit = 2
    while bit < blocks:
        queries = jnp.concatenate([queries, exchange(queries, sizes, blk=bit)], axis=0)
        order += [(b ^ bit, x) for b, x in order]
        bit *= 2
    near = [(b, x) for x in range(spans) for b in range(min(blocks, 2))]
    others = [exchange(queries, sizes, blk=b, wide=x) for b, x in near[:0:-1]]
    queries = stack([queries] + others[::-1])
    order = [(b ^ c, x ^ y) for c, y in near for b, x in order]
    order = tuple((b, x, flip) for flip in range(2) for b, x in order)
    return scores(order, wide, lows, queries, swap(queries, sizes, {"wide": 1}), grad_store)


def solution(mesh):
    return jax.shard_map(
        functools.partial(on_device, dict(mesh.shape)),
        mesh=mesh,
        in_specs=(
            P("blk", ("grp", "wide")),
            P("blk", ("grp", "wide")),
            P(("grp", "wide"), None),
            P(("grp", "wide"), None),
            P(),
            P(),
            P(("grp", "wide", "blk"), None),
        ),
        out_specs=P(None, ("grp", "wide", "blk")),
        check_vma=False,
    )
```

```python
import functools
import itertools

import jax
import jax.numpy as jnp
from jax import lax
from jax.experimental import pallas as pl
from jax.experimental.pallas import tpu as pltpu
from jax.sharding import PartitionSpec as P

SEQ = 32
VMEM = pl.BlockSpec(memory_space=pltpu.VMEM)
HBM = pl.BlockSpec(memory_space=pltpu.HBM)
MIB = 1 << 20
PROJECT_VMEM = 55_889_920
HIGH = 12


def contract(lhs, rhs, left, right):
    return lax.dot_general(
        lhs, rhs, (((left,), (right,)), ((), ())), preferred_element_type=jnp.float32
    )


def two_parts(value):
    high = value.astype(jnp.bfloat16)
    return high, (value - high.astype(jnp.float32)).astype(jnp.bfloat16)


def odd_bits(value):
    for shift in (16, 8, 4, 2, 1):
        value = value ^ (value >> shift)
    return value & 1


def exchange(value, sizes, wide=0, grp=0, blk=0):
    flip = odd_bits(wide) ^ odd_bits(grp >> 1)
    return swap(value, sizes, {"wide": 2 * wide + flip, "grp": grp, "blk": blk})


def swap(value, sizes, far):
    axes = tuple(sizes)
    coordinates = list(itertools.product(*(range(sizes[a]) for a in axes)))
    index = {c: i for i, c in enumerate(coordinates)}
    pairs = [
        (i, index[tuple(p ^ far.get(a, 0) for p, a in zip(c, axes))])
        for c, i in index.items()
    ]
    return lax.ppermute(value, axes, pairs)


def own_half():
    slot, group = lax.axis_index("wide"), lax.axis_index("grp")
    return lax.rem(slot, 2) ^ odd_bits(slot // 2) ^ odd_bits(group // 2)


def project_kernel(width_in, acts, grads, proj, given, kept, act_buf, grad_buf, sems):
    slices, tokens = given.shape[0], given.shape[2]
    half, x = own_half(), lax.axis_index("wide") // 2
    copies = []
    for k in range(2 * slices):
        first = ((x ^ (k % slices)) * 2 + (half ^ (k < slices))) * tokens
        rows = pl.ds(pl.multiple_of(first, tokens), tokens)
        for source, target, part in ((acts, act_buf, 0), (grads, grad_buf, 1)):
            copy = pltpu.make_async_copy(source.at[rows], target.at[k], sems.at[k, part])
            copy.start()
            copies.append(copy)
    for k in range(2 * slices):
        copies[2 * k].wait()
        copies[2 * k + 1].wait()
        out = given if k < slices else kept
        out[k % slices, :width_in] = contract(proj[:width_in], act_buf[k], 1, 1)
        out[k % slices, width_in:] = contract(proj[width_in:], grad_buf[k], 1, 1)


def project(slices, acts, grads, proj, width_in):
    tokens, features = acts.shape[0] // (2 * slices), acts.shape[1]
    width = proj.shape[0]
    out = jax.ShapeDtypeStruct((slices, width, tokens), jnp.float32)
    return pl.pallas_call(
        functools.partial(project_kernel, width_in),
        out_shape=(out, out),
        in_specs=[HBM] * 2 + [VMEM],
        out_specs=(VMEM, VMEM),
        scratch_shapes=[
            pltpu.VMEM((2 * slices, tokens, features), jnp.bfloat16),
            pltpu.VMEM((2 * slices, tokens, features), jnp.bfloat16),
            pltpu.SemaphoreType.DMA((2 * slices, 2)),
        ],
        compiler_params=pltpu.CompilerParams(vmem_limit_bytes=PROJECT_VMEM),
        cost_estimate=pl.CostEstimate(
            flops=4 * slices * tokens * features * width,
            bytes_accessed=8 * slices * tokens * features,
            transcendentals=0,
        ),
    )(acts, grads, proj)


def spread_kernel(in_inverse, out_inverse, spread_out, spread_in):
    width_out, width_in = out_inverse.shape[0], in_inverse.shape[0]
    columns, lanes = spread_out.shape[1], spread_in.shape[1]
    row = lax.broadcasted_iota(jnp.int32, (width_out, columns), 0)
    column = lax.broadcasted_iota(jnp.int32, (width_out, columns), 1)
    start = row * width_in
    repeat = ((column >= start) & (column < start + width_in)).astype(jnp.bfloat16)
    high, low = two_parts(out_inverse[...])
    high = contract(high, repeat, 0, 0).astype(jnp.bfloat16)
    low = contract(low, repeat, 0, 0).astype(jnp.bfloat16)
    spread_out[...] = jnp.concatenate([high, low, high, low], axis=0)
    row = lax.broadcasted_iota(jnp.int32, (width_in, lanes), 0)
    column = lax.broadcasted_iota(jnp.int32, (width_in, lanes), 1)
    tile = (lax.rem(column, width_in) == row).astype(jnp.bfloat16)
    high, low = two_parts(in_inverse[...])
    high = contract(high, tile, 1, 0).astype(jnp.bfloat16)
    low = contract(low, tile, 1, 0).astype(jnp.bfloat16)
    spread_in[...] = jnp.concatenate([high, low, high, low], axis=0)


def spread_inverses(in_inverse, out_inverse):
    width_in, width_out = in_inverse.shape[0], out_inverse.shape[0]
    return pl.pallas_call(
        spread_kernel,
        out_shape=(
            jax.ShapeDtypeStruct((4 * width_out, width_out * width_in), jnp.bfloat16),
            jax.ShapeDtypeStruct((4 * width_in, 128), jnp.bfloat16),
        ),
        in_specs=[VMEM, VMEM],
        out_specs=(VMEM, VMEM),
        compiler_params=pltpu.CompilerParams(vmem_limit_bytes=8 * MIB),
        cost_estimate=pl.CostEstimate(flops=1 << 33, bytes_accessed=16 * MIB, transcendentals=0),
    )(in_inverse, out_inverse)


def query_kernel(summed, spread_out, spread_in, out):
    width_in = spread_in.shape[0] // 4
    tokens = summed.shape[1]
    queries, columns = out.shape
    lanes = spread_in.shape[1]
    low = summed[...].T
    in_high, in_low = two_parts(low[:, :width_in])
    out_high, out_low = two_parts(low[:, width_in:])
    side_in = jnp.concatenate([in_high, in_high, in_low, in_low], axis=1)
    side_out = jnp.concatenate([out_high, out_high, out_low, out_low], axis=1)
    spread_in_low = contract(side_in, spread_in[...], 1, 0)
    step = 256
    wide = jnp.concatenate([spread_in_low] * (step // lanes), axis=1)
    for start in range(0, columns, step):
        part = contract(side_out, spread_out[:, start : start + step], 1, 0) * wide
        part = jnp.sum(part.reshape(queries, tokens // queries, step), axis=1)
        out[:, start : start + step] = part.astype(out.dtype)


def build_queries(summed, spread_out, spread_in):
    tokens = summed.shape[1]
    return pl.pallas_call(
        query_kernel,
        out_shape=jax.ShapeDtypeStruct((tokens // SEQ, spread_out.shape[1]), jnp.bfloat16),
        in_specs=[VMEM] * 3,
        out_specs=VMEM,
        compiler_params=pltpu.CompilerParams(vmem_limit_bytes=12 * MIB),
        cost_estimate=pl.CostEstimate(flops=1 << 33, bytes_accessed=16 * MIB, transcendentals=0),
    )(summed, spread_out, spread_in)


def score_kernel(order, wide, held, got, store, out):
    blk, x, half = lax.axis_index("blk"), lax.axis_index("wide") // 2, own_half()
    queries = jnp.concatenate([held[...], got[...]], axis=0)
    rows = out.shape[0] // len(order)
    targets = [
        pl.multiple_of((((blk ^ far_blk) * (wide // 2) + (x ^ far_x)) * 2 + (half ^ flip)) * rows, rows)
        for far_blk, far_x, flip in order
    ]
    step = 512
    for start in range(0, out.shape[1], step):
        part = contract(queries, store[start : start + step], 1, 1)
        for r, row in enumerate(targets):
            out[pl.ds(row, rows), start : start + step] = part[r * rows : (r + 1) * rows]


def scores(order, wide, held, got, store):
    return pl.pallas_call(
        functools.partial(score_kernel, order, wide),
        out_shape=jax.ShapeDtypeStruct((2 * held.shape[0], store.shape[0]), jnp.float32),
        in_specs=[VMEM] * 3,
        out_specs=VMEM,
        compiler_params=pltpu.CompilerParams(vmem_limit_bytes=20 * MIB),
    )(held, got, store)


def stack(pieces):
    rows = pieces[0].shape[0]
    zero = jnp.zeros((), pieces[0].dtype)
    return sum(
        lax.pad(piece, zero, ((n * rows, (len(pieces) - 1 - n) * rows, 0), (0, 0, 0)))
        for n, piece in enumerate(pieces)
    )


def encode(value, width_in):
    exponents = [
        jnp.clip(jnp.ceil(jnp.log2(jnp.max(jnp.abs(part), axis=0, keepdims=True))), -100, 100)
        for part in (value[:width_in], value[width_in:])
    ]
    rows = value.shape[0]
    row = lax.broadcasted_iota(jnp.int32, (rows + 2, 1), 0)
    exponent = jnp.where(row < width_in, *exponents)
    scaled = lax.pad(value, jnp.float32(0), ((0, 2, 0), (0, 0, 0))) * jnp.exp2(HIGH - exponent)
    scaled = jnp.where(row == rows, exponents[0], jnp.where(row > rows, exponents[1], scaled))
    return scaled.astype(jnp.float16)


def decode(value, width_in):
    rows = value.shape[0] - 2
    value = value.astype(jnp.float32)
    row = lax.broadcasted_iota(jnp.int32, (rows, 1), 0)
    exponent = jnp.where(row < width_in, value[rows : rows + 1], value[rows + 1 :])
    return value[:rows] * jnp.exp2(exponent - HIGH)


def on_device(
    sizes, activations, out_grads, in_projection, out_projection, in_inverse, out_inverse, grad_store
):
    wide, groups, blocks = sizes["wide"], sizes["grp"], sizes["blk"]
    slices, lows, width_in = wide // 2, min(groups, 2), in_inverse.shape[0]
    proj = jnp.concatenate([in_projection.T, out_projection.T], axis=0)
    given, kept = project(slices, activations, out_grads, proj, width_in)
    both = kept + swap(given, sizes, {"wide": 1})
    held = both[0]
    coded = [encode(part, width_in) for part in both]
    for k in range(slices * lows - 1, 0, -1):
        got = exchange(coded[k // lows], sizes, wide=k // lows, grp=k % lows)
        held = held + decode(got, width_in)
    bit = lows
    while bit < groups:
        held = held + decode(exchange(encode(held, width_in), sizes, grp=bit), width_in)
        bit *= 2
    spread_out, spread_in = spread_inverses(in_inverse, out_inverse)
    queries = build_queries(held, spread_out, spread_in)
    order = [(0, 0)]
    bit = 2
    while bit < blocks:
        queries = stack([queries, exchange(queries, sizes, blk=bit)])
        order += [(b ^ bit, x) for b, x in order]
        bit *= 2
    near = [(b, x) for x in range(slices) for b in range(min(blocks, 2))]
    others = [exchange(queries, sizes, blk=b, wide=x) for b, x in near[:0:-1]]
    queries = stack([queries] + others[::-1])
    order = [(b ^ c, x ^ y) for c, y in near for b, x in order]
    order = tuple((b, x, flip) for flip in range(2) for b, x in order)
    return scores(order, wide, queries, swap(queries, sizes, {"wide": 1}), grad_store)


def solution(mesh):
    return jax.shard_map(
        functools.partial(on_device, dict(mesh.shape)),
        mesh=mesh,
        in_specs=(
            P("blk", ("grp", "wide")),
            P("blk", ("grp", "wide")),
            P(("grp", "wide"), None),
            P(("grp", "wide"), None),
            P(),
            P(),
            P(("grp", "wide", "blk"), None),
        ),
        out_specs=P(None, ("grp", "wide", "blk")),
        check_vma=False,
    )
```

```python
import functools
import itertools

import jax
import jax.numpy as jnp
from jax import lax
from jax.experimental import pallas as pl
from jax.experimental.pallas import tpu as pltpu
from jax.sharding import PartitionSpec as P

SEQ = 32
VMEM = pl.BlockSpec(memory_space=pltpu.VMEM)
HBM = pl.BlockSpec(memory_space=pltpu.HBM)
MIB = 1 << 20
PROJECT_VMEM = 55_889_920
CROSS = (-1, -2, -1)
HIGH = 12


def contract(lhs, rhs, left, right):
    return lax.dot_general(
        lhs, rhs, (((left,), (right,)), ((), ())), preferred_element_type=jnp.float32
    )


def two_parts(value):
    high = value.astype(jnp.bfloat16)
    return high, (value - high.astype(jnp.float32)).astype(jnp.bfloat16)


def odd_bits(value):
    for shift in (16, 8, 4, 2, 1):
        value = value ^ (value >> shift)
    return value & 1


def exchange(value, sizes, wide=0, grp=0, blk=0):
    flip = odd_bits(wide & CROSS[0]) ^ odd_bits(grp & CROSS[1]) ^ odd_bits(blk & CROSS[2])
    return swap(value, sizes, {"wide": 2 * wide + flip, "grp": grp, "blk": blk})


def swap(value, sizes, far):
    axes = tuple(sizes)
    coordinates = list(itertools.product(*(range(sizes[a]) for a in axes)))
    index = {c: i for i, c in enumerate(coordinates)}
    pairs = [
        (i, index[tuple(p ^ far.get(a, 0) for p, a in zip(c, axes))])
        for c, i in index.items()
    ]
    return lax.ppermute(value, axes, pairs)


def own_half():
    slot = lax.axis_index("wide")
    half = lax.rem(slot, 2)
    for value, mask in zip((slot // 2, lax.axis_index("grp"), lax.axis_index("blk")), CROSS):
        half = half ^ odd_bits(value & mask)
    return half


def project_kernel(width_in, acts, grads, proj, given, kept, act_buf, grad_buf, sems):
    slices, tokens = given.shape[0], given.shape[2]
    half, x = own_half(), lax.axis_index("wide") // 2
    copies = []
    for k in range(2 * slices):
        first = ((x ^ (k % slices)) * 2 + (half ^ (k < slices))) * tokens
        rows = pl.ds(pl.multiple_of(first, tokens), tokens)
        for source, target, part in ((acts, act_buf, 0), (grads, grad_buf, 1)):
            copy = pltpu.make_async_copy(source.at[rows], target.at[k], sems.at[k, part])
            copy.start()
            copies.append(copy)
    for k in range(2 * slices):
        copies[2 * k].wait()
        copies[2 * k + 1].wait()
        out = given if k < slices else kept
        out[k % slices, :width_in] = contract(proj[:width_in], act_buf[k], 1, 1)
        out[k % slices, width_in:] = contract(proj[width_in:], grad_buf[k], 1, 1)


def project(slices, acts, grads, proj, width_in):
    tokens, features = acts.shape[0] // (2 * slices), acts.shape[1]
    width = proj.shape[0]
    out = jax.ShapeDtypeStruct((slices, width, tokens), jnp.float32)
    return pl.pallas_call(
        functools.partial(project_kernel, width_in),
        out_shape=(out, out),
        in_specs=[HBM] * 2 + [VMEM],
        out_specs=(VMEM, VMEM),
        scratch_shapes=[
            pltpu.VMEM((2 * slices, tokens, features), jnp.bfloat16),
            pltpu.VMEM((2 * slices, tokens, features), jnp.bfloat16),
            pltpu.SemaphoreType.DMA((2 * slices, 2)),
        ],
        compiler_params=pltpu.CompilerParams(vmem_limit_bytes=PROJECT_VMEM),
        cost_estimate=pl.CostEstimate(
            flops=4 * slices * tokens * features * width,
            bytes_accessed=8 * slices * tokens * features,
            transcendentals=0,
        ),
    )(acts, grads, proj)


def spread_kernel(in_inverse, out_inverse, spread_out, spread_in):
    width_out, width_in = out_inverse.shape[0], in_inverse.shape[0]
    columns, lanes = spread_out.shape[1], spread_in.shape[1]
    row = lax.broadcasted_iota(jnp.int32, (width_out, columns), 0)
    column = lax.broadcasted_iota(jnp.int32, (width_out, columns), 1)
    start = row * width_in
    repeat = ((column >= start) & (column < start + width_in)).astype(jnp.bfloat16)
    high, low = two_parts(out_inverse[...])
    high = contract(high, repeat, 0, 0).astype(jnp.bfloat16)
    low = contract(low, repeat, 0, 0).astype(jnp.bfloat16)
    spread_out[...] = jnp.concatenate([high, low, high, low], axis=0)
    row = lax.broadcasted_iota(jnp.int32, (width_in, lanes), 0)
    column = lax.broadcasted_iota(jnp.int32, (width_in, lanes), 1)
    tile = (lax.rem(column, width_in) == row).astype(jnp.bfloat16)
    high, low = two_parts(in_inverse[...])
    high = contract(high, tile, 1, 0).astype(jnp.bfloat16)
    low = contract(low, tile, 1, 0).astype(jnp.bfloat16)
    spread_in[...] = jnp.concatenate([high, low, high, low], axis=0)


def spread_inverses(in_inverse, out_inverse):
    width_in, width_out = in_inverse.shape[0], out_inverse.shape[0]
    return pl.pallas_call(
        spread_kernel,
        out_shape=(
            jax.ShapeDtypeStruct((4 * width_out, width_out * width_in), jnp.bfloat16),
            jax.ShapeDtypeStruct((4 * width_in, 128), jnp.bfloat16),
        ),
        in_specs=[VMEM, VMEM],
        out_specs=(VMEM, VMEM),
        compiler_params=pltpu.CompilerParams(vmem_limit_bytes=8 * MIB),
        cost_estimate=pl.CostEstimate(flops=1 << 33, bytes_accessed=16 * MIB, transcendentals=0),
    )(in_inverse, out_inverse)


def query_kernel(summed, spread_out, spread_in, out):
    width_in = spread_in.shape[0] // 4
    tokens = summed.shape[1]
    queries, columns = out.shape
    lanes = spread_in.shape[1]
    low = summed[...].T
    in_high, in_low = two_parts(low[:, :width_in])
    out_high, out_low = two_parts(low[:, width_in:])
    side_in = jnp.concatenate([in_high, in_high, in_low, in_low], axis=1)
    side_out = jnp.concatenate([out_high, out_high, out_low, out_low], axis=1)
    spread_in_low = contract(side_in, spread_in[...], 1, 0)
    step = 256
    wide = jnp.concatenate([spread_in_low] * (step // lanes), axis=1)
    for start in range(0, columns, step):
        part = contract(side_out, spread_out[:, start : start + step], 1, 0) * wide
        part = jnp.sum(part.reshape(queries, tokens // queries, step), axis=1)
        out[:, start : start + step] = part.astype(out.dtype)


def build_queries(summed, spread_out, spread_in):
    tokens = summed.shape[1]
    return pl.pallas_call(
        query_kernel,
        out_shape=jax.ShapeDtypeStruct((tokens // SEQ, spread_out.shape[1]), jnp.bfloat16),
        in_specs=[VMEM] * 3,
        out_specs=VMEM,
        compiler_params=pltpu.CompilerParams(vmem_limit_bytes=12 * MIB),
        cost_estimate=pl.CostEstimate(flops=1 << 33, bytes_accessed=16 * MIB, transcendentals=0),
    )(summed, spread_out, spread_in)


def score_kernel(order, wide, held, got, store, out, part, sems):
    blk, x, half = lax.axis_index("blk"), lax.axis_index("wide") // 2, own_half()
    queries = jnp.concatenate([held[...], got[...]], axis=0)
    rows = out.shape[0] // len(order)
    targets = [
        pl.multiple_of((((blk ^ far_blk) * (wide // 2) + (x ^ far_x)) * 2 + (half ^ flip)) * rows, rows)
        for far_blk, far_x, flip in order
    ]
    step = 512
    stores = []
    for n, start in enumerate(range(0, out.shape[1], step)):
        columns = pl.ds(start, step)
        product = contract(store[columns], queries, 1, 1).T
        for r, row in enumerate(targets):
            part[pl.ds(row, rows), columns] = product[r * rows : (r + 1) * rows]
        stores.append(pltpu.make_async_copy(part.at[:, columns], out.at[:, columns], sems.at[n]))
        stores[-1].start()
    for copy in stores:
        copy.wait()


def scores(order, wide, held, got, store):
    return pl.pallas_call(
        functools.partial(score_kernel, order, wide),
        out_shape=jax.ShapeDtypeStruct((2 * held.shape[0], store.shape[0]), jnp.float32),
        in_specs=[VMEM] * 3,
        out_specs=HBM,
        scratch_shapes=[
            pltpu.VMEM((2 * held.shape[0], store.shape[0]), jnp.float32),
            pltpu.SemaphoreType.DMA((pl.cdiv(store.shape[0], 512),)),
        ],
        compiler_params=pltpu.CompilerParams(vmem_limit_bytes=20 * MIB),
    )(held, got, store)


def stack(pieces):
    rows = pieces[0].shape[0]
    zero = jnp.zeros((), pieces[0].dtype)
    return sum(
        lax.pad(piece, zero, ((n * rows, (len(pieces) - 1 - n) * rows, 0), (0, 0, 0)))
        for n, piece in enumerate(pieces)
    )


def encode(value, width_in):
    exponents = [
        jnp.clip(jnp.ceil(jnp.log2(jnp.max(jnp.abs(part), axis=0, keepdims=True))), -100, 100)
        for part in (value[:width_in], value[width_in:])
    ]
    rows = value.shape[0]
    row = lax.broadcasted_iota(jnp.int32, (rows + 2, 1), 0)
    exponent = jnp.where(row < width_in, *exponents)
    scaled = lax.pad(value, jnp.float32(0), ((0, 2, 0), (0, 0, 0))) * jnp.exp2(HIGH - exponent)
    scaled = jnp.where(row == rows, exponents[0], jnp.where(row > rows, exponents[1], scaled))
    return scaled.astype(jnp.float16)


def decode(value, width_in):
    rows = value.shape[0] - 2
    value = value.astype(jnp.float32)
    row = lax.broadcasted_iota(jnp.int32, (rows, 1), 0)
    exponent = jnp.where(row < width_in, value[rows : rows + 1], value[rows + 1 :])
    return value[:rows] * jnp.exp2(exponent - HIGH)


def on_device(
    sizes, activations, out_grads, in_projection, out_projection, in_inverse, out_inverse, grad_store
):
    wide, groups, blocks = sizes["wide"], sizes["grp"], sizes["blk"]
    slices, lows, width_in = wide // 2, min(groups, 2), in_inverse.shape[0]
    proj = jnp.concatenate([in_projection.T, out_projection.T], axis=0)
    given, kept = project(slices, activations, out_grads, proj, width_in)
    both = kept + swap(given, sizes, {"wide": 1})
    held = both[0]
    coded = [encode(part, width_in) for part in both]
    for k in range(slices * lows - 1, 0, -1):
        got = exchange(coded[k // lows], sizes, wide=k // lows, grp=k % lows)
        held = held + decode(got, width_in)
    bit = lows
    while bit < groups:
        held = held + decode(exchange(encode(held, width_in), sizes, grp=bit), width_in)
        bit *= 2
    spread_out, spread_in = spread_inverses(in_inverse, out_inverse)
    queries = build_queries(held, spread_out, spread_in)
    order = [(0, 0)]
    bit = 2
    while bit < blocks:
        queries = stack([queries, exchange(queries, sizes, blk=bit)])
        order += [(b ^ bit, x) for b, x in order]
        bit *= 2
    near = [(b, x) for x in range(slices) for b in range(min(blocks, 2))]
    others = [exchange(queries, sizes, blk=b, wide=x) for b, x in near[:0:-1]]
    queries = stack([queries] + others[::-1])
    order = [(b ^ c, x ^ y) for c, y in near for b, x in order]
    order = tuple((b, x, flip) for flip in range(2) for b, x in order)
    return scores(order, wide, queries, swap(queries, sizes, {"wide": 1}), grad_store)


def solution(mesh):
    return jax.shard_map(
        functools.partial(on_device, dict(mesh.shape)),
        mesh=mesh,
        in_specs=(
            P("blk", ("grp", "wide")),
            P("blk", ("grp", "wide")),
            P(("grp", "wide"), None),
            P(("grp", "wide"), None),
            P(),
            P(),
            P(("grp", "wide", "blk"), None),
        ),
        out_specs=P(None, ("grp", "wide", "blk")),
        check_vma=False,
    )
```

```python
import functools
import itertools
import math

import jax
import jax.numpy as jnp
from jax import lax
from jax.experimental import pallas as pl
from jax.experimental.pallas import tpu as pltpu
from jax.sharding import PartitionSpec as P

SEQ = 32
VMEM = pl.BlockSpec(memory_space=pltpu.VMEM)
HBM = pl.BlockSpec(memory_space=pltpu.HBM)
MIB = 1 << 20
PROJECT_VMEM = 55_889_920
CROSS = (-1, -2, 0)
HIGH = 12


def contract(lhs, rhs, left, right):
    return lax.dot_general(
        lhs, rhs, (((left,), (right,)), ((), ())), preferred_element_type=jnp.float32
    )


def two_parts(value):
    high = value.astype(jnp.bfloat16)
    return high, (value - high.astype(jnp.float32)).astype(jnp.bfloat16)


def odd_bits(value):
    for shift in (16, 8, 4, 2, 1):
        value = value ^ (value >> shift)
    return value & 1


def exchange(value, sizes, wide=0, grp=0, blk=0):
    flip = odd_bits(wide & CROSS[0]) ^ odd_bits(grp & CROSS[1]) ^ odd_bits(blk & CROSS[2])
    return swap(value, sizes, {"wide": 2 * wide + flip, "grp": grp, "blk": blk})


def swap(value, sizes, far):
    axes = tuple(sizes)
    coordinates = list(itertools.product(*(range(sizes[a]) for a in axes)))
    index = {c: i for i, c in enumerate(coordinates)}
    pairs = [
        (i, index[tuple(p ^ far.get(a, 0) for p, a in zip(c, axes))])
        for c, i in index.items()
    ]
    return lax.ppermute(value, axes, pairs)


def own_half():
    slot = lax.axis_index("wide")
    half = lax.rem(slot, 2)
    for value, mask in zip((slot // 2, lax.axis_index("grp"), lax.axis_index("blk")), CROSS):
        half = half ^ odd_bits(value & mask)
    return half


def project_kernel(width_in, acts, grads, proj, given, kept, act_buf, grad_buf, sems):
    slices, tokens = given.shape[0], given.shape[2]
    half, x = own_half(), lax.axis_index("wide") // 2
    copies = []
    for k in range(2 * slices):
        first = ((x ^ (k % slices)) * 2 + (half ^ (k < slices))) * tokens
        rows = pl.ds(pl.multiple_of(first, tokens), tokens)
        for source, target, part in ((acts, act_buf, 0), (grads, grad_buf, 1)):
            copy = pltpu.make_async_copy(source.at[rows], target.at[k], sems.at[k, part])
            copy.start()
            copies.append(copy)
    for k in range(2 * slices):
        copies[2 * k].wait()
        copies[2 * k + 1].wait()
        out = given if k < slices else kept
        out[k % slices, :width_in] = contract(proj[:width_in], act_buf[k], 1, 1)
        out[k % slices, width_in:] = contract(proj[width_in:], grad_buf[k], 1, 1)


def project(slices, acts, grads, proj, width_in):
    tokens, features = acts.shape[0] // (2 * slices), acts.shape[1]
    width = proj.shape[0]
    out = jax.ShapeDtypeStruct((slices, width, tokens), jnp.float32)
    return pl.pallas_call(
        functools.partial(project_kernel, width_in),
        out_shape=(out, out),
        in_specs=[HBM] * 2 + [VMEM],
        out_specs=(VMEM, VMEM),
        scratch_shapes=[
            pltpu.VMEM((2 * slices, tokens, features), jnp.bfloat16),
            pltpu.VMEM((2 * slices, tokens, features), jnp.bfloat16),
            pltpu.SemaphoreType.DMA((2 * slices, 2)),
        ],
        compiler_params=pltpu.CompilerParams(vmem_limit_bytes=PROJECT_VMEM),
        cost_estimate=pl.CostEstimate(
            flops=4 * slices * tokens * features * width,
            bytes_accessed=8 * slices * tokens * features,
            transcendentals=0,
        ),
    )(acts, grads, proj)


def spread_kernel(in_inverse, out_inverse, spread_out, spread_in):
    width_out, width_in = out_inverse.shape[0], in_inverse.shape[0]
    columns, lanes = spread_out.shape[1], spread_in.shape[1]
    row = lax.broadcasted_iota(jnp.int32, (width_out, columns), 0)
    column = lax.broadcasted_iota(jnp.int32, (width_out, columns), 1)
    start = row * width_in
    repeat = ((column >= start) & (column < start + width_in)).astype(jnp.bfloat16)
    high, low = two_parts(out_inverse[...])
    high = contract(high, repeat, 0, 0).astype(jnp.bfloat16)
    low = contract(low, repeat, 0, 0).astype(jnp.bfloat16)
    spread_out[...] = jnp.concatenate([high, low, high, low], axis=0)
    row = lax.broadcasted_iota(jnp.int32, (width_in, lanes), 0)
    column = lax.broadcasted_iota(jnp.int32, (width_in, lanes), 1)
    tile = (lax.rem(column, width_in) == row).astype(jnp.bfloat16)
    high, low = two_parts(in_inverse[...])
    high = contract(high, tile, 1, 0).astype(jnp.bfloat16)
    low = contract(low, tile, 1, 0).astype(jnp.bfloat16)
    spread_in[...] = jnp.concatenate([high, low, high, low], axis=0)


def spread_inverses(in_inverse, out_inverse):
    width_in, width_out = in_inverse.shape[0], out_inverse.shape[0]
    return pl.pallas_call(
        spread_kernel,
        out_shape=(
            jax.ShapeDtypeStruct((4 * width_out, width_out * width_in), jnp.bfloat16),
            jax.ShapeDtypeStruct((4 * width_in, 128), jnp.bfloat16),
        ),
        in_specs=[VMEM, VMEM],
        out_specs=(VMEM, VMEM),
        compiler_params=pltpu.CompilerParams(vmem_limit_bytes=8 * MIB),
        cost_estimate=pl.CostEstimate(flops=1 << 33, bytes_accessed=16 * MIB, transcendentals=0),
    )(in_inverse, out_inverse)


def query_kernel(summed, spread_out, spread_in, out):
    width_in = spread_in.shape[0] // 4
    tokens = summed.shape[1]
    queries, columns = out.shape
    lanes = spread_in.shape[1]
    low = summed[...].T
    in_high, in_low = two_parts(low[:, :width_in])
    out_high, out_low = two_parts(low[:, width_in:])
    side_in = jnp.concatenate([in_high, in_high, in_low, in_low], axis=1)
    side_out = jnp.concatenate([out_high, out_high, out_low, out_low], axis=1)
    spread_in_low = contract(side_in, spread_in[...], 1, 0)
    step = math.gcd(columns, 256)
    wide = jnp.concatenate([spread_in_low] * (step // lanes), axis=1)
    for start in range(0, columns, step):
        part = contract(side_out, spread_out[:, start : start + step], 1, 0) * wide
        part = jnp.sum(part.reshape(queries, tokens // queries, step), axis=1)
        out[:, start : start + step] = part.astype(out.dtype)


def build_queries(summed, spread_out, spread_in):
    tokens = summed.shape[1]
    return pl.pallas_call(
        query_kernel,
        out_shape=jax.ShapeDtypeStruct((tokens // SEQ, spread_out.shape[1]), jnp.bfloat16),
        in_specs=[VMEM] * 3,
        out_specs=VMEM,
        compiler_params=pltpu.CompilerParams(vmem_limit_bytes=12 * MIB),
        cost_estimate=pl.CostEstimate(flops=1 << 33, bytes_accessed=16 * MIB, transcendentals=0),
    )(summed, spread_out, spread_in)


def score_kernel(order, wide, held, got, store, out, part, sems):
    blk, x, half = lax.axis_index("blk"), lax.axis_index("wide") // 2, own_half()
    queries = jnp.concatenate([held[...], got[...]], axis=0)
    rows = out.shape[0] // len(order)
    targets = [
        pl.multiple_of((((blk ^ far_blk) * (wide // 2) + (x ^ far_x)) * 2 + (half ^ flip)) * rows, rows)
        for far_blk, far_x, flip in order
    ]
    step = math.gcd(out.shape[1], 512)
    stores = []
    for n, start in enumerate(range(0, out.shape[1], step)):
        columns = pl.ds(start, step)
        product = contract(store[columns], queries, 1, 1).T
        for r, row in enumerate(targets):
            part[pl.ds(row, rows), columns] = product[r * rows : (r + 1) * rows]
        stores.append(pltpu.make_async_copy(part.at[:, columns], out.at[:, columns], sems.at[n]))
        stores[-1].start()
    for copy in stores:
        copy.wait()


def scores(order, wide, held, got, store):
    return pl.pallas_call(
        functools.partial(score_kernel, order, wide),
        out_shape=jax.ShapeDtypeStruct((2 * held.shape[0], store.shape[0]), jnp.float32),
        in_specs=[VMEM] * 3,
        out_specs=HBM,
        scratch_shapes=[
            pltpu.VMEM((2 * held.shape[0], store.shape[0]), jnp.float32),
            pltpu.SemaphoreType.DMA((store.shape[0] // math.gcd(store.shape[0], 512),)),
        ],
        compiler_params=pltpu.CompilerParams(vmem_limit_bytes=20 * MIB),
    )(held, got, store)


def pad_rows(piece, place, places):
    rows, zero = piece.shape[0], jnp.zeros((), piece.dtype)
    return lax.pad(piece, zero, ((place * rows, (places - 1 - place) * rows, 0), (0, 0, 0)))


def encode(value, width_in):
    exponents = [
        jnp.clip(jnp.ceil(jnp.log2(jnp.max(jnp.abs(part), axis=0, keepdims=True))), -100, 100)
        for part in (value[:width_in], value[width_in:])
    ]
    rows = value.shape[0]
    row = lax.broadcasted_iota(jnp.int32, (rows + 2, 1), 0)
    exponent = jnp.where(row < width_in, *exponents)
    scaled = lax.pad(value, jnp.float32(0), ((0, 2, 0), (0, 0, 0))) * jnp.exp2(HIGH - exponent)
    scaled = jnp.where(row == rows, exponents[0], jnp.where(row > rows, exponents[1], scaled))
    return scaled.astype(jnp.float16)


def decode(value, width_in):
    rows = value.shape[0] - 2
    value = value.astype(jnp.float32)
    row = lax.broadcasted_iota(jnp.int32, (rows, 1), 0)
    exponent = jnp.where(row < width_in, value[rows : rows + 1], value[rows + 1 :])
    return value[:rows] * jnp.exp2(exponent - HIGH)


def on_device(
    sizes, activations, out_grads, in_projection, out_projection, in_inverse, out_inverse, grad_store
):
    wide, groups, blocks = sizes["wide"], sizes["grp"], sizes["blk"]
    slices, lows, width_in = wide // 2, min(groups, 2), in_inverse.shape[0]
    proj = jnp.concatenate([in_projection.T, out_projection.T], axis=0)
    given, kept = project(slices, activations, out_grads, proj, width_in)
    both = kept + swap(given, sizes, {"wide": 1})
    held = both[0]
    coded = [encode(part, width_in) for part in both]
    for k in range(slices * lows - 1, 0, -1):
        got = exchange(coded[k // lows], sizes, wide=k // lows, grp=k % lows)
        held = held + decode(got, width_in)
    bit = lows
    while bit < groups:
        held = held + decode(exchange(encode(held, width_in), sizes, grp=bit), width_in)
        bit *= 2
    spread_out, spread_in = spread_inverses(in_inverse, out_inverse)
    queries = build_queries(held, spread_out, spread_in)
    order = [(0, 0)]
    bit = 2
    while bit < blocks:
        queries = pad_rows(queries, 0, 2) + pad_rows(exchange(queries, sizes, blk=bit), 1, 2)
        order += [(b ^ bit, x) for b, x in order]
        bit *= 2
    near = [(b, x) for x in range(slices) for b in range(min(blocks, 2))]
    others = [exchange(queries, sizes, blk=b, wide=x) for b, x in near[:0:-1]]
    queries = pad_rows(queries, 0, len(near))
    for n, other in zip(range(len(near) - 1, 0, -1), others):
        queries = lax.optimization_barrier(queries + pad_rows(other, n, len(near)))
    order = [(b ^ c, x ^ y) for c, y in near for b, x in order]
    order = tuple((b, x, flip) for flip in range(2) for b, x in order)
    return scores(order, wide, queries, swap(queries, sizes, {"wide": 1}), grad_store)


def solution(mesh):
    return jax.shard_map(
        functools.partial(on_device, dict(mesh.shape)),
        mesh=mesh,
        in_specs=(
            P("blk", ("grp", "wide")),
            P("blk", ("grp", "wide")),
            P(("grp", "wide"), None),
            P(("grp", "wide"), None),
            P(),
            P(),
            P(("grp", "wide", "blk"), None),
        ),
        out_specs=P(None, ("grp", "wide", "blk")),
        check_vma=False,
    )
```

```python
import functools
import itertools
import math

import jax
import jax.numpy as jnp
from jax import lax
from jax.experimental import pallas as pl
from jax.experimental.pallas import tpu as pltpu
from jax.sharding import PartitionSpec as P

SEQ = 32
VMEM = pl.BlockSpec(memory_space=pltpu.VMEM)
HBM = pl.BlockSpec(memory_space=pltpu.HBM)
MIB = 1 << 20
PROJECT_VMEM = 55_889_920
CROSS = (-1, -2, 0)
HIGH = 12


def contract(lhs, rhs, left, right):
    return lax.dot_general(
        lhs, rhs, (((left,), (right,)), ((), ())), preferred_element_type=jnp.float32
    )


def two_parts(value):
    high = value.astype(jnp.bfloat16)
    return high, (value - high.astype(jnp.float32)).astype(jnp.bfloat16)


def odd_bits(value):
    for shift in (16, 8, 4, 2, 1):
        value = value ^ (value >> shift)
    return value & 1


def exchange(value, sizes, wide=0, grp=0, blk=0):
    flip = odd_bits(wide & CROSS[0]) ^ odd_bits(grp & CROSS[1]) ^ odd_bits(blk & CROSS[2])
    return swap(value, sizes, {"wide": 2 * wide + flip, "grp": grp, "blk": blk})


def swap(value, sizes, far):
    axes = tuple(sizes)
    coordinates = list(itertools.product(*(range(sizes[a]) for a in axes)))
    index = {c: i for i, c in enumerate(coordinates)}
    pairs = [
        (i, index[tuple(p ^ far.get(a, 0) for p, a in zip(c, axes))])
        for c, i in index.items()
    ]
    return lax.ppermute(value, axes, pairs)


def own_half():
    slot = lax.axis_index("wide")
    half = lax.rem(slot, 2)
    for value, mask in zip((slot // 2, lax.axis_index("grp"), lax.axis_index("blk")), CROSS):
        half = half ^ odd_bits(value & mask)
    return half


def project_kernel(width_in, acts, grads, proj, given, kept, act_buf, grad_buf, sems):
    slices, tokens = given.shape[0], given.shape[2]
    half, x = own_half(), lax.axis_index("wide") // 2
    copies = []
    for k in range(2 * slices):
        first = ((x ^ (k % slices)) * 2 + (half ^ (k < slices))) * tokens
        rows = pl.ds(pl.multiple_of(first, tokens), tokens)
        for source, target, part in ((acts, act_buf, 0), (grads, grad_buf, 1)):
            copy = pltpu.make_async_copy(source.at[rows], target.at[k], sems.at[k, part])
            copy.start()
            copies.append(copy)
    for k in range(2 * slices):
        if k % slices == 0:
            for copy in copies[2 * k : 2 * (k + slices)]:
                copy.wait()
        out = given if k < slices else kept
        out[k % slices, :width_in] = contract(proj[:width_in], act_buf[k], 1, 1)
        out[k % slices, width_in:] = contract(proj[width_in:], grad_buf[k], 1, 1)


def project(slices, acts, grads, proj, width_in):
    tokens, features = acts.shape[0] // (2 * slices), acts.shape[1]
    width = proj.shape[0]
    out = jax.ShapeDtypeStruct((slices, width, tokens), jnp.float32)
    return pl.pallas_call(
        functools.partial(project_kernel, width_in),
        out_shape=(out, out),
        in_specs=[HBM] * 2 + [VMEM],
        out_specs=(VMEM, VMEM),
        scratch_shapes=[
            pltpu.VMEM((2 * slices, tokens, features), jnp.bfloat16),
            pltpu.VMEM((2 * slices, tokens, features), jnp.bfloat16),
            pltpu.SemaphoreType.DMA((2 * slices, 2)),
        ],
        compiler_params=pltpu.CompilerParams(vmem_limit_bytes=PROJECT_VMEM),
        cost_estimate=pl.CostEstimate(
            flops=4 * slices * tokens * features * width,
            bytes_accessed=8 * slices * tokens * features,
            transcendentals=0,
        ),
    )(acts, grads, proj)


def spread_kernel(in_inverse, out_inverse, spread_out, spread_in):
    width_out, width_in = out_inverse.shape[0], in_inverse.shape[0]
    columns, lanes = spread_out.shape[1], spread_in.shape[1]
    row = lax.broadcasted_iota(jnp.int32, (width_out, columns), 0)
    column = lax.broadcasted_iota(jnp.int32, (width_out, columns), 1)
    start = row * width_in
    repeat = ((column >= start) & (column < start + width_in)).astype(jnp.bfloat16)
    high, low = two_parts(out_inverse[...])
    high = contract(high, repeat, 0, 0).astype(jnp.bfloat16)
    low = contract(low, repeat, 0, 0).astype(jnp.bfloat16)
    spread_out[...] = jnp.concatenate([high, low, high, low], axis=0)
    row = lax.broadcasted_iota(jnp.int32, (width_in, lanes), 0)
    column = lax.broadcasted_iota(jnp.int32, (width_in, lanes), 1)
    tile = (lax.rem(column, width_in) == row).astype(jnp.bfloat16)
    high, low = two_parts(in_inverse[...])
    high = contract(high, tile, 1, 0).astype(jnp.bfloat16)
    low = contract(low, tile, 1, 0).astype(jnp.bfloat16)
    spread_in[...] = jnp.concatenate([high, low, high, low], axis=0)


def spread_inverses(in_inverse, out_inverse):
    width_in, width_out = in_inverse.shape[0], out_inverse.shape[0]
    return pl.pallas_call(
        spread_kernel,
        out_shape=(
            jax.ShapeDtypeStruct((4 * width_out, width_out * width_in), jnp.bfloat16),
            jax.ShapeDtypeStruct((4 * width_in, 128), jnp.bfloat16),
        ),
        in_specs=[VMEM, VMEM],
        out_specs=(VMEM, VMEM),
        compiler_params=pltpu.CompilerParams(vmem_limit_bytes=8 * MIB),
        cost_estimate=pl.CostEstimate(flops=1 << 33, bytes_accessed=16 * MIB, transcendentals=0),
    )(in_inverse, out_inverse)


def query_kernel(summed, spread_out, spread_in, out):
    width_in = spread_in.shape[0] // 4
    tokens = summed.shape[1]
    queries, columns = out.shape
    lanes = spread_in.shape[1]
    in_high, in_low = two_parts(summed[:width_in])
    out_high, out_low = two_parts(summed[width_in:])
    side_in = jnp.concatenate([in_high, in_high, in_low, in_low], axis=0)
    side_out = jnp.concatenate([out_high, out_high, out_low, out_low], axis=0).T
    spread_in_low = contract(side_in, spread_in[...], 0, 0)
    step = math.gcd(columns, 256)
    wide = jnp.concatenate([spread_in_low] * (step // lanes), axis=1)
    for start in range(0, columns, step):
        part = contract(side_out, spread_out[:, start : start + step], 1, 0) * wide
        part = jnp.sum(part.reshape(queries, tokens // queries, step), axis=1)
        out[:, start : start + step] = part.astype(out.dtype)


def build_queries(summed, spread_out, spread_in):
    tokens = summed.shape[1]
    return pl.pallas_call(
        query_kernel,
        out_shape=jax.ShapeDtypeStruct((tokens // SEQ, spread_out.shape[1]), jnp.bfloat16),
        in_specs=[VMEM] * 3,
        out_specs=VMEM,
        compiler_params=pltpu.CompilerParams(vmem_limit_bytes=12 * MIB),
        cost_estimate=pl.CostEstimate(flops=1 << 33, bytes_accessed=16 * MIB, transcendentals=0),
    )(summed, spread_out, spread_in)


def score_kernel(order, wide, held, got, store, out, part, sems):
    blk, x, half = lax.axis_index("blk"), lax.axis_index("wide") // 2, own_half()
    queries = jnp.concatenate([held[...], got[...]], axis=0)
    rows = out.shape[0] // len(order)
    targets = [
        pl.multiple_of((((blk ^ far_blk) * (wide // 2) + (x ^ far_x)) * 2 + (half ^ flip)) * rows, rows)
        for far_blk, far_x, flip in order
    ]
    step = math.gcd(out.shape[1], 512)
    stores = []
    for n, start in enumerate(range(0, out.shape[1], step)):
        columns = pl.ds(start, step)
        product = contract(store[columns], queries, 1, 1).T
        for r, row in enumerate(targets):
            part[pl.ds(row, rows), columns] = product[r * rows : (r + 1) * rows]
        stores.append(pltpu.make_async_copy(part.at[:, columns], out.at[:, columns], sems.at[n]))
        stores[-1].start()
    for copy in stores:
        copy.wait()


def scores(order, wide, held, got, store):
    return pl.pallas_call(
        functools.partial(score_kernel, order, wide),
        out_shape=jax.ShapeDtypeStruct((2 * held.shape[0], store.shape[0]), jnp.float32),
        in_specs=[VMEM] * 3,
        out_specs=HBM,
        scratch_shapes=[
            pltpu.VMEM((2 * held.shape[0], store.shape[0]), jnp.float32),
            pltpu.SemaphoreType.DMA((store.shape[0] // math.gcd(store.shape[0], 512),)),
        ],
        compiler_params=pltpu.CompilerParams(vmem_limit_bytes=20 * MIB),
    )(held, got, store)


def pad_rows(piece, place, places):
    rows, zero = piece.shape[0], jnp.zeros((), piece.dtype)
    return lax.pad(piece, zero, ((place * rows, (places - 1 - place) * rows, 0), (0, 0, 0)))


def encode(value, width_in):
    exponents = [
        jnp.clip(jnp.ceil(jnp.log2(jnp.max(jnp.abs(part), axis=0, keepdims=True))), -100, 100)
        for part in (value[:width_in], value[width_in:])
    ]
    rows = value.shape[0]
    row = lax.broadcasted_iota(jnp.int32, (rows + 2, 1), 0)
    exponent = jnp.where(row < width_in, *exponents)
    scaled = lax.pad(value, jnp.float32(0), ((0, 2, 0), (0, 0, 0))) * jnp.exp2(HIGH - exponent)
    scaled = jnp.where(row == rows, exponents[0], jnp.where(row > rows, exponents[1], scaled))
    return scaled.astype(jnp.float16)


def decode(value, width_in):
    rows = value.shape[0] - 2
    value = value.astype(jnp.float32)
    row = lax.broadcasted_iota(jnp.int32, (rows, 1), 0)
    exponent = jnp.where(row < width_in, value[rows : rows + 1], value[rows + 1 :])
    return value[:rows] * jnp.exp2(exponent - HIGH)


def on_device(
    sizes, activations, out_grads, in_projection, out_projection, in_inverse, out_inverse, grad_store
):
    wide, groups, blocks = sizes["wide"], sizes["grp"], sizes["blk"]
    slices, lows, width_in = wide // 2, min(groups, 2), in_inverse.shape[0]
    proj = jnp.concatenate([in_projection.T, out_projection.T], axis=0)
    given, kept = project(slices, activations, out_grads, proj, width_in)
    both = kept + swap(given, sizes, {"wide": 1})
    held = both[0]
    coded = [encode(part, width_in) for part in both]
    for k in range(slices * lows - 1, 0, -1):
        got = exchange(coded[k // lows], sizes, wide=k // lows, grp=k % lows)
        held = held + decode(got, width_in)
    bit = lows
    while bit < groups:
        held = held + decode(exchange(encode(held, width_in), sizes, grp=bit), width_in)
        bit *= 2
    spread_out, spread_in = spread_inverses(in_inverse, out_inverse)
    queries = build_queries(held, spread_out, spread_in)
    order = [(0, 0)]
    bit = 2
    while bit < blocks:
        queries = pad_rows(queries, 0, 2) + pad_rows(exchange(queries, sizes, blk=bit), 1, 2)
        order += [(b ^ bit, x) for b, x in order]
        bit *= 2
    near = [(b, x) for x in range(slices) for b in range(min(blocks, 2))]
    others = [exchange(queries, sizes, blk=b, wide=x) for b, x in near[:0:-1]]
    queries = pad_rows(queries, 0, len(near))
    for n, other in zip(range(len(near) - 1, 0, -1), others):
        queries = lax.optimization_barrier(queries + pad_rows(other, n, len(near)))
    order = [(b ^ c, x ^ y) for c, y in near for b, x in order]
    order = tuple((b, x, flip) for flip in range(2) for b, x in order)
    return scores(order, wide, queries, swap(queries, sizes, {"wide": 1}), grad_store)


def solution(mesh):
    return jax.shard_map(
        functools.partial(on_device, dict(mesh.shape)),
        mesh=mesh,
        in_specs=(
            P("blk", ("grp", "wide")),
            P("blk", ("grp", "wide")),
            P(("grp", "wide"), None),
            P(("grp", "wide"), None),
            P(),
            P(),
            P(("grp", "wide", "blk"), None),
        ),
        out_specs=P(None, ("grp", "wide", "blk")),
        check_vma=False,
    )
```

```python
import functools
import itertools
import math

import jax
import jax.numpy as jnp
from jax import lax
from jax.experimental import pallas as pl
from jax.experimental.pallas import tpu as pltpu
from jax.sharding import PartitionSpec as P

SEQ = 32
VMEM = pl.BlockSpec(memory_space=pltpu.VMEM)
HBM = pl.BlockSpec(memory_space=pltpu.HBM)
MIB = 1 << 20
PROJECT_VMEM = 55_889_920
CROSS = (-1, -2, 0)
HIGH = 12


def contract(lhs, rhs, left, right):
    return lax.dot_general(
        lhs, rhs, (((left,), (right,)), ((), ())), preferred_element_type=jnp.float32
    )


def two_parts(value):
    high = value.astype(jnp.bfloat16)
    return high, (value - high.astype(jnp.float32)).astype(jnp.bfloat16)


def odd_bits(value):
    for shift in (16, 8, 4, 2, 1):
        value = value ^ (value >> shift)
    return value & 1


def exchange(value, sizes, wide=0, grp=0, blk=0):
    flip = odd_bits(wide & CROSS[0]) ^ odd_bits(grp & CROSS[1]) ^ odd_bits(blk & CROSS[2])
    return swap(value, sizes, {"wide": 2 * wide + flip, "grp": grp, "blk": blk})


def swap(value, sizes, far):
    axes = tuple(sizes)
    coordinates = list(itertools.product(*(range(sizes[a]) for a in axes)))
    index = {c: i for i, c in enumerate(coordinates)}
    pairs = [
        (i, index[tuple(p ^ far.get(a, 0) for p, a in zip(c, axes))])
        for c, i in index.items()
    ]
    return lax.ppermute(value, axes, pairs)


def own_half():
    slot = lax.axis_index("wide")
    half = lax.rem(slot, 2)
    for value, mask in zip((slot // 2, lax.axis_index("grp"), lax.axis_index("blk")), CROSS):
        half = half ^ odd_bits(value & mask)
    return half


def project_kernel(width_in, acts, grads, proj, given, kept, act_buf, grad_buf, sems):
    slices, tokens = given.shape[0], given.shape[2]
    half, x = own_half(), lax.axis_index("wide") // 2
    copies = []
    for k in range(2 * slices):
        first = ((x ^ (k % slices)) * 2 + (half ^ (k < slices))) * tokens
        rows = pl.ds(pl.multiple_of(first, tokens), tokens)
        for source, target, part in ((acts, act_buf, 0), (grads, grad_buf, 1)):
            copy = pltpu.make_async_copy(source.at[rows], target.at[k], sems.at[k, part])
            copy.start()
            copies.append(copy)
    for k in range(2 * slices):
        if k % slices == 0:
            for copy in copies[2 * k : 2 * (k + slices)]:
                copy.wait()
        out = given if k < slices else kept
        out[k % slices, :width_in] = contract(proj[:width_in], act_buf[k], 1, 1)
        out[k % slices, width_in:] = contract(proj[width_in:], grad_buf[k], 1, 1)


def project(slices, acts, grads, proj, width_in):
    tokens, features = acts.shape[0] // (2 * slices), acts.shape[1]
    width = proj.shape[0]
    out = jax.ShapeDtypeStruct((slices, width, tokens), jnp.float32)
    return pl.pallas_call(
        functools.partial(project_kernel, width_in),
        out_shape=(out, out),
        in_specs=[HBM] * 2 + [VMEM],
        out_specs=(VMEM, VMEM),
        scratch_shapes=[
            pltpu.VMEM((2 * slices, tokens, features), jnp.bfloat16),
            pltpu.VMEM((2 * slices, tokens, features), jnp.bfloat16),
            pltpu.SemaphoreType.DMA((2 * slices, 2)),
        ],
        compiler_params=pltpu.CompilerParams(vmem_limit_bytes=PROJECT_VMEM),
        cost_estimate=pl.CostEstimate(
            flops=4 * slices * tokens * features * width,
            bytes_accessed=8 * slices * tokens * features,
            transcendentals=0,
        ),
    )(acts, grads, proj)


def spread_kernel(in_inverse, out_inverse, spread_out, spread_in):
    width_out, width_in = out_inverse.shape[0], in_inverse.shape[0]
    columns, lanes = spread_out.shape[1], spread_in.shape[1]
    row = lax.broadcasted_iota(jnp.int32, (width_out, columns), 0)
    column = lax.broadcasted_iota(jnp.int32, (width_out, columns), 1)
    start = row * width_in
    repeat = ((column >= start) & (column < start + width_in)).astype(jnp.bfloat16)
    high, low = two_parts(out_inverse[...])
    high = contract(high, repeat, 0, 0).astype(jnp.bfloat16)
    low = contract(low, repeat, 0, 0).astype(jnp.bfloat16)
    spread_out[...] = jnp.concatenate([high, low, high, low], axis=0)
    row = lax.broadcasted_iota(jnp.int32, (width_in, lanes), 0)
    column = lax.broadcasted_iota(jnp.int32, (width_in, lanes), 1)
    tile = (lax.rem(column, width_in) == row).astype(jnp.bfloat16)
    high, low = two_parts(in_inverse[...])
    high = contract(high, tile, 1, 0).astype(jnp.bfloat16)
    low = contract(low, tile, 1, 0).astype(jnp.bfloat16)
    spread_in[...] = jnp.concatenate([high, low, high, low], axis=0)


def spread_inverses(in_inverse, out_inverse):
    width_in, width_out = in_inverse.shape[0], out_inverse.shape[0]
    return pl.pallas_call(
        spread_kernel,
        out_shape=(
            jax.ShapeDtypeStruct((4 * width_out, width_out * width_in), jnp.bfloat16),
            jax.ShapeDtypeStruct((4 * width_in, 128), jnp.bfloat16),
        ),
        in_specs=[VMEM, VMEM],
        out_specs=(VMEM, VMEM),
        compiler_params=pltpu.CompilerParams(vmem_limit_bytes=8 * MIB),
        cost_estimate=pl.CostEstimate(flops=1 << 33, bytes_accessed=16 * MIB, transcendentals=0),
    )(in_inverse, out_inverse)


def query_kernel(summed, spread_out, spread_in, out):
    width_in = spread_in.shape[0] // 4
    tokens = summed.shape[1]
    queries, columns = out.shape
    lanes = spread_in.shape[1]
    in_high, in_low = two_parts(summed[:width_in])
    out_high, out_low = two_parts(summed[width_in:])
    side_in = jnp.concatenate([in_high, in_high, in_low, in_low], axis=0)
    side_out = jnp.concatenate([out_high, out_high, out_low, out_low], axis=0).T
    spread_in_low = contract(side_in, spread_in[...], 0, 0)
    step = math.gcd(columns, 256)
    wide = jnp.concatenate([spread_in_low] * (step // lanes), axis=1)
    for start in range(0, columns, step):
        part = contract(side_out, spread_out[:, start : start + step], 1, 0) * wide
        part = jnp.sum(part.reshape(queries, tokens // queries, step), axis=1)
        out[:, start : start + step] = part.astype(out.dtype)


def build_queries(summed, spread_out, spread_in):
    tokens = summed.shape[1]
    return pl.pallas_call(
        query_kernel,
        out_shape=jax.ShapeDtypeStruct((tokens // SEQ, spread_out.shape[1]), jnp.bfloat16),
        in_specs=[VMEM] * 3,
        out_specs=VMEM,
        compiler_params=pltpu.CompilerParams(vmem_limit_bytes=12 * MIB),
        cost_estimate=pl.CostEstimate(flops=1 << 33, bytes_accessed=16 * MIB, transcendentals=0),
    )(summed, spread_out, spread_in)


def score_kernel(order, wide, pieces, *refs):
    blk, x, half = lax.axis_index("blk"), lax.axis_index("wide") // 2, own_half()
    store, out, part, sems = refs[pieces:]
    queries = jnp.concatenate([ref[...] for ref in refs[:pieces]], axis=0)
    rows = out.shape[0] // len(order)
    targets = [
        pl.multiple_of((((blk ^ far_blk) * (wide // 2) + (x ^ far_x)) * 2 + (half ^ flip)) * rows, rows)
        for far_blk, far_x, flip in order
    ]
    step = math.gcd(out.shape[1], 512)
    stores = []
    for n, start in enumerate(range(0, out.shape[1], step)):
        columns = pl.ds(start, step)
        product = contract(store[columns], queries, 1, 1).T
        for r, row in enumerate(targets):
            part[pl.ds(row, rows), columns] = product[r * rows : (r + 1) * rows]
        stores.append(pltpu.make_async_copy(part.at[:, columns], out.at[:, columns], sems.at[n]))
        stores[-1].start()
    for copy in stores:
        copy.wait()


def scores(order, wide, held, got, store):
    return pl.pallas_call(
        functools.partial(score_kernel, order, wide, len(held) + len(got)),
        out_shape=jax.ShapeDtypeStruct((2 * sum(piece.shape[0] for piece in held), store.shape[0]), jnp.float32),
        in_specs=[VMEM] * (len(held) + len(got) + 1),
        out_specs=HBM,
        scratch_shapes=[
            pltpu.VMEM((2 * sum(piece.shape[0] for piece in held), store.shape[0]), jnp.float32),
            pltpu.SemaphoreType.DMA((store.shape[0] // math.gcd(store.shape[0], 512),)),
        ],
        compiler_params=pltpu.CompilerParams(vmem_limit_bytes=20 * MIB),
    )(*held, *got, store)


def pad_rows(piece, place, places):
    rows, zero = piece.shape[0], jnp.zeros((), piece.dtype)
    return lax.pad(piece, zero, ((place * rows, (places - 1 - place) * rows, 0), (0, 0, 0)))


def stack(pieces):
    return sum(pad_rows(piece, n, len(pieces)) for n, piece in enumerate(pieces))


def encode(value, width_in):
    exponents = [
        jnp.clip(jnp.ceil(jnp.log2(jnp.max(jnp.abs(part), axis=0, keepdims=True))), -100, 100)
        for part in (value[:width_in], value[width_in:])
    ]
    rows = value.shape[0]
    row = lax.broadcasted_iota(jnp.int32, (rows + 2, 1), 0)
    exponent = jnp.where(row < width_in, *exponents)
    scaled = lax.pad(value, jnp.float32(0), ((0, 2, 0), (0, 0, 0))) * jnp.exp2(HIGH - exponent)
    scaled = jnp.where(row == rows, exponents[0], jnp.where(row > rows, exponents[1], scaled))
    return scaled.astype(jnp.float16)


def decode(value, width_in):
    rows = value.shape[0] - 2
    value = value.astype(jnp.float32)
    row = lax.broadcasted_iota(jnp.int32, (rows, 1), 0)
    exponent = jnp.where(row < width_in, value[rows : rows + 1], value[rows + 1 :])
    return value[:rows] * jnp.exp2(exponent - HIGH)


def on_device(
    sizes, activations, out_grads, in_projection, out_projection, in_inverse, out_inverse, grad_store
):
    wide, groups, blocks = sizes["wide"], sizes["grp"], sizes["blk"]
    slices, lows, width_in = wide // 2, min(groups, 2), in_inverse.shape[0]
    proj = jnp.concatenate([in_projection.T, out_projection.T], axis=0)
    given, kept = project(slices, activations, out_grads, proj, width_in)
    both = kept + swap(given, sizes, {"wide": 1})
    held = both[0]
    coded = [encode(part, width_in) for part in both]
    for k in range(slices * lows - 1, 0, -1):
        got = exchange(coded[k // lows], sizes, wide=k // lows, grp=k % lows)
        held = held + decode(got, width_in)
    bit = lows
    while bit < groups:
        held = held + decode(exchange(encode(held, width_in), sizes, grp=bit), width_in)
        bit *= 2
    spread_out, spread_in = spread_inverses(in_inverse, out_inverse)
    queries = build_queries(held, spread_out, spread_in)
    order = [(0, 0)]
    bit = 2
    while bit < blocks:
        queries = pad_rows(queries, 0, 2) + pad_rows(exchange(queries, sizes, blk=bit), 1, 2)
        order += [(b ^ bit, x) for b, x in order]
        bit *= 2
    near = [(b, x) for x in range(slices) for b in range(min(blocks, 2))]
    others = [exchange(queries, sizes, blk=b, wide=x) for b, x in near[:0:-1]]
    pieces, passed, orders = [queries], [], [order]
    for (c, y), other in zip(near[:0:-1], others):
        pieces.append(other)
        orders.append([(b ^ c, x ^ y) for b, x in order])
    early = lax.optimization_barrier(stack(pieces[:2]))
    late = stack(pieces[2:]) if pieces[2:] else None
    held = [early] + ([late] if pieces[2:] else [])
    passed = [swap(piece, sizes, {"wide": 1}) for piece in held]
    order = tuple((b, x, flip) for flip in range(2) for part in orders for b, x in part)
    return scores(order, wide, held, passed, grad_store)


def solution(mesh):
    return jax.shard_map(
        functools.partial(on_device, dict(mesh.shape)),
        mesh=mesh,
        in_specs=(
            P("blk", ("grp", "wide")),
            P("blk", ("grp", "wide")),
            P(("grp", "wide"), None),
            P(("grp", "wide"), None),
            P(),
            P(),
            P(("grp", "wide", "blk"), None),
        ),
        out_specs=P(None, ("grp", "wide", "blk")),
        check_vma=False,
    )
```

```python
import functools
import itertools
import math

import jax
import jax.numpy as jnp
from jax import lax
from jax.experimental import pallas as pl
from jax.experimental.pallas import tpu as pltpu
from jax.sharding import PartitionSpec as P

SEQ = 32
VMEM = pl.BlockSpec(memory_space=pltpu.VMEM)
HBM = pl.BlockSpec(memory_space=pltpu.HBM)
MIB = 1 << 20
PROJECT_VMEM = 55_889_920
CROSS = (-1, -2, 0)
HIGH = 12


def contract(lhs, rhs, left, right):
    return lax.dot_general(
        lhs, rhs, (((left,), (right,)), ((), ())), preferred_element_type=jnp.float32
    )


def two_parts(value):
    high = value.astype(jnp.bfloat16)
    return high, (value - high.astype(jnp.float32)).astype(jnp.bfloat16)


def odd_bits(value):
    for shift in (16, 8, 4, 2, 1):
        value = value ^ (value >> shift)
    return value & 1


def exchange(value, sizes, wide=0, grp=0, blk=0):
    flip = odd_bits(wide & CROSS[0]) ^ odd_bits(grp & CROSS[1]) ^ odd_bits(blk & CROSS[2])
    return swap(value, sizes, {"wide": 2 * wide + flip, "grp": grp, "blk": blk})


def swap(value, sizes, far):
    axes = tuple(sizes)
    coordinates = list(itertools.product(*(range(sizes[a]) for a in axes)))
    index = {c: i for i, c in enumerate(coordinates)}
    pairs = [
        (i, index[tuple(p ^ far.get(a, 0) for p, a in zip(c, axes))])
        for c, i in index.items()
    ]
    return lax.ppermute(value, axes, pairs)


def own_half():
    slot = lax.axis_index("wide")
    half = lax.rem(slot, 2)
    for value, mask in zip((slot // 2, lax.axis_index("grp"), lax.axis_index("blk")), CROSS):
        half = half ^ odd_bits(value & mask)
    return half


def project_kernel(width_in, acts, grads, proj, given, kept, act_buf, grad_buf, sems):
    slices, tokens = given.shape[0], given.shape[2]
    half, x = own_half(), lax.axis_index("wide") // 2
    copies = []
    for k in range(2 * slices):
        first = ((x ^ (k % slices)) * 2 + (half ^ (k < slices))) * tokens
        rows = pl.ds(pl.multiple_of(first, tokens), tokens)
        for source, target, part in ((acts, act_buf, 0), (grads, grad_buf, 1)):
            copy = pltpu.make_async_copy(source.at[rows], target.at[k], sems.at[k, part])
            copy.start()
            copies.append(copy)
    for k in range(2 * slices):
        if k % slices == 0:
            for copy in copies[2 * k : 2 * (k + slices)]:
                copy.wait()
        out = given if k < slices else kept
        out[k % slices, :width_in] = contract(proj[:width_in], act_buf[k], 1, 1)
        out[k % slices, width_in:] = contract(proj[width_in:], grad_buf[k], 1, 1)


def project(slices, acts, grads, proj, width_in):
    tokens, features = acts.shape[0] // (2 * slices), acts.shape[1]
    width = proj.shape[0]
    out = jax.ShapeDtypeStruct((slices, width, tokens), jnp.float32)
    return pl.pallas_call(
        functools.partial(project_kernel, width_in),
        out_shape=(out, out),
        in_specs=[HBM] * 2 + [VMEM],
        out_specs=(VMEM, VMEM),
        scratch_shapes=[
            pltpu.VMEM((2 * slices, tokens, features), jnp.bfloat16),
            pltpu.VMEM((2 * slices, tokens, features), jnp.bfloat16),
            pltpu.SemaphoreType.DMA((2 * slices, 2)),
        ],
        compiler_params=pltpu.CompilerParams(vmem_limit_bytes=PROJECT_VMEM),
        cost_estimate=pl.CostEstimate(
            flops=1 << 30,
            bytes_accessed=8 * slices * tokens * features,
            transcendentals=0,
        ),
    )(acts, grads, proj)


def spread_kernel(in_inverse, out_inverse, spread_out, spread_in):
    width_out, width_in = out_inverse.shape[0], in_inverse.shape[0]
    columns, lanes = spread_out.shape[1], spread_in.shape[1]
    row = lax.broadcasted_iota(jnp.int32, (width_out, columns), 0)
    column = lax.broadcasted_iota(jnp.int32, (width_out, columns), 1)
    start = row * width_in
    repeat = ((column >= start) & (column < start + width_in)).astype(jnp.bfloat16)
    high, low = two_parts(out_inverse[...])
    high = contract(high, repeat, 0, 0).astype(jnp.bfloat16)
    low = contract(low, repeat, 0, 0).astype(jnp.bfloat16)
    spread_out[...] = jnp.concatenate([high, low, high, low], axis=0)
    row = lax.broadcasted_iota(jnp.int32, (width_in, lanes), 0)
    column = lax.broadcasted_iota(jnp.int32, (width_in, lanes), 1)
    tile = (lax.rem(column, width_in) == row).astype(jnp.bfloat16)
    high, low = two_parts(in_inverse[...])
    high = contract(high, tile, 1, 0).astype(jnp.bfloat16)
    low = contract(low, tile, 1, 0).astype(jnp.bfloat16)
    spread_in[...] = jnp.concatenate([high, low, high, low], axis=0)


def spread_inverses(in_inverse, out_inverse):
    width_in, width_out = in_inverse.shape[0], out_inverse.shape[0]
    return pl.pallas_call(
        spread_kernel,
        out_shape=(
            jax.ShapeDtypeStruct((4 * width_out, width_out * width_in), jnp.bfloat16),
            jax.ShapeDtypeStruct((4 * width_in, 128), jnp.bfloat16),
        ),
        in_specs=[VMEM, VMEM],
        out_specs=(VMEM, VMEM),
        compiler_params=pltpu.CompilerParams(vmem_limit_bytes=8 * MIB),
        cost_estimate=pl.CostEstimate(flops=1 << 33, bytes_accessed=16 * MIB, transcendentals=0),
    )(in_inverse, out_inverse)


def query_kernel(summed, spread_out, spread_in, out):
    width_in = spread_in.shape[0] // 4
    tokens = summed.shape[1]
    queries, columns = out.shape
    lanes = spread_in.shape[1]
    in_high, in_low = two_parts(summed[:width_in])
    out_high, out_low = two_parts(summed[width_in:])
    side_in = jnp.concatenate([in_high, in_high, in_low, in_low], axis=0)
    side_out = jnp.concatenate([out_high, out_high, out_low, out_low], axis=0).T
    spread_in_low = contract(side_in, spread_in[...], 0, 0)
    step = math.gcd(columns, 256)
    wide = jnp.concatenate([spread_in_low] * (step // lanes), axis=1)
    for start in range(0, columns, step):
        part = contract(side_out, spread_out[:, start : start + step], 1, 0) * wide
        part = jnp.sum(part.reshape(queries, tokens // queries, step), axis=1)
        out[:, start : start + step] = part.astype(out.dtype)


def build_queries(summed, spread_out, spread_in):
    tokens = summed.shape[1]
    return pl.pallas_call(
        query_kernel,
        out_shape=jax.ShapeDtypeStruct((tokens // SEQ, spread_out.shape[1]), jnp.bfloat16),
        in_specs=[VMEM] * 3,
        out_specs=VMEM,
        compiler_params=pltpu.CompilerParams(vmem_limit_bytes=12 * MIB),
        cost_estimate=pl.CostEstimate(flops=1 << 33, bytes_accessed=16 * MIB, transcendentals=0),
    )(summed, spread_out, spread_in)


def score_kernel(order, wide, pieces, *refs):
    blk, x, half = lax.axis_index("blk"), lax.axis_index("wide") // 2, own_half()
    store, out, part, sems = refs[pieces:]
    queries = jnp.concatenate([ref[...] for ref in refs[:pieces]], axis=0)
    rows = out.shape[0] // len(order)
    targets = [
        pl.multiple_of((((blk ^ far_blk) * (wide // 2) + (x ^ far_x)) * 2 + (half ^ flip)) * rows, rows)
        for far_blk, far_x, flip in order
    ]
    step = math.gcd(out.shape[1], 512)
    stores = []
    for n, start in enumerate(range(0, out.shape[1], step)):
        columns = pl.ds(start, step)
        product = contract(store[columns], queries, 1, 1).T
        for r, row in enumerate(targets):
            part[pl.ds(row, rows), columns] = product[r * rows : (r + 1) * rows]
        stores.append(pltpu.make_async_copy(part.at[:, columns], out.at[:, columns], sems.at[n]))
        stores[-1].start()
    for copy in stores:
        copy.wait()


def scores(order, wide, held, got, store):
    return pl.pallas_call(
        functools.partial(score_kernel, order, wide, len(held) + len(got)),
        out_shape=jax.ShapeDtypeStruct((2 * sum(piece.shape[0] for piece in held), store.shape[0]), jnp.float32),
        in_specs=[VMEM] * (len(held) + len(got) + 1),
        out_specs=HBM,
        scratch_shapes=[
            pltpu.VMEM((2 * sum(piece.shape[0] for piece in held), store.shape[0]), jnp.float32),
            pltpu.SemaphoreType.DMA((store.shape[0] // math.gcd(store.shape[0], 512),)),
        ],
        compiler_params=pltpu.CompilerParams(vmem_limit_bytes=20 * MIB),
    )(*held, *got, store)


def pad_rows(piece, place, places):
    rows, zero = piece.shape[0], jnp.zeros((), piece.dtype)
    return lax.pad(piece, zero, ((place * rows, (places - 1 - place) * rows, 0), (0, 0, 0)))


def stack(pieces):
    return sum(pad_rows(piece, n, len(pieces)) for n, piece in enumerate(pieces))


def encode(value, width_in):
    exponents = [
        jnp.clip(jnp.ceil(jnp.log2(jnp.max(jnp.abs(part), axis=0, keepdims=True))), -100, 100)
        for part in (value[:width_in], value[width_in:])
    ]
    rows = value.shape[0]
    row = lax.broadcasted_iota(jnp.int32, (rows + 2, 1), 0)
    exponent = jnp.where(row < width_in, *exponents)
    scaled = lax.pad(value, jnp.float32(0), ((0, 2, 0), (0, 0, 0))) * jnp.exp2(HIGH - exponent)
    scaled = jnp.where(row == rows, exponents[0], jnp.where(row > rows, exponents[1], scaled))
    return scaled.astype(jnp.float16)


def decode(value, width_in):
    rows = value.shape[0] - 2
    value = value.astype(jnp.float32)
    row = lax.broadcasted_iota(jnp.int32, (rows, 1), 0)
    exponent = jnp.where(row < width_in, value[rows : rows + 1], value[rows + 1 :])
    return value[:rows] * jnp.exp2(exponent - HIGH)


def on_device(
    sizes, activations, out_grads, in_projection, out_projection, in_inverse, out_inverse, grad_store
):
    wide, groups, blocks = sizes["wide"], sizes["grp"], sizes["blk"]
    slices, lows, width_in = wide // 2, min(groups, 2), in_inverse.shape[0]
    proj = jnp.concatenate([in_projection.T, out_projection.T], axis=0)
    given, kept = project(slices, activations, out_grads, proj, width_in)
    both = kept + swap(given, sizes, {"wide": 1})
    held = both[0]
    coded = [encode(part, width_in) for part in both]
    for k in range(slices * lows - 1, 0, -1):
        got = exchange(coded[k // lows], sizes, wide=k // lows, grp=k % lows)
        held = held + decode(got, width_in)
    bit = lows
    while bit < groups:
        held = held + decode(exchange(encode(held, width_in), sizes, grp=bit), width_in)
        bit *= 2
    spread_out, spread_in = spread_inverses(in_inverse, out_inverse)
    queries = build_queries(held, spread_out, spread_in)
    order = [(0, 0)]
    bit = 2
    while bit < blocks:
        queries = pad_rows(queries, 0, 2) + pad_rows(exchange(queries, sizes, blk=bit), 1, 2)
        order += [(b ^ bit, x) for b, x in order]
        bit *= 2
    near = [(b, x) for x in range(slices) for b in range(min(blocks, 2))]
    others = [exchange(queries, sizes, blk=b, wide=x) for b, x in near[:0:-1]]
    pieces, passed, orders = [queries], [], [order]
    for (c, y), other in zip(near[:0:-1], others):
        pieces.append(other)
        orders.append([(b ^ c, x ^ y) for b, x in order])
    early = lax.optimization_barrier(stack(pieces[:2]))
    late = stack(pieces[2:]) if pieces[2:] else None
    held = [early] + ([late] if pieces[2:] else [])
    passed = [swap(piece, sizes, {"wide": 1}) for piece in held]
    order = tuple((b, x, flip) for flip in range(2) for part in orders for b, x in part)
    return scores(order, wide, held, passed, grad_store)


def solution(mesh):
    return jax.shard_map(
        functools.partial(on_device, dict(mesh.shape)),
        mesh=mesh,
        in_specs=(
            P("blk", ("grp", "wide")),
            P("blk", ("grp", "wide")),
            P(("grp", "wide"), None),
            P(("grp", "wide"), None),
            P(),
            P(),
            P(("grp", "wide", "blk"), None),
        ),
        out_specs=P(None, ("grp", "wide", "blk")),
        check_vma=False,
    )
```
